128 devices in a mesh: sec: 2 (over core), dev: 64 (over y, x, z).
Axes of the slice: x: 4, y: 4, z: 4, core: 2. Of those that a mesh axis runs over, the one named last changes fastest.
Arguments:
- queries: bfloat16 [512, 128, 576], P('dev', 'sec'), may hold values from -11 to 11
- cache: bfloat16 [512, 256, 576], P('dev'), may hold values from -2.2 to 2.2
- lengths: int32 [512], P('dev'), may hold values from 1 to 256, 65536 in all
- hidden_rows: bfloat16 [1024, 7168], P(('sec', 'dev')), may hold values from -6 to 6
- routes: int32 [1024, 8], P(('sec', 'dev')), may hold values from 0 to 31, all different within a row; in each aligned block of 8 rows (0 to 7, 8 to 15, ...) at most 3 rows name the same one
- gate_codes: int32 [1024, 8], P(('sec', 'dev')), may hold values from 1 to 65535
- placement: int32 [32], replicated, may hold values from 0 to 31, each once
- w_gate_up: bfloat16 [2, 7168, 65536], P(None, None, ('sec', 'dev')), may hold values from -0.0625 to 0.0625
- w_down: bfloat16 [65536, 7168], P(('sec', 'dev')), may hold values from -0.125 to 0.125
Outputs:
- context: bfloat16 [512, 128, 512], P('dev', 'sec')
- mixed: bfloat16 [1024, 7168], P(('sec', 'dev'))
The draws below stay inside these ranges and needn't reach their ends.
Inputs may be any that keep to these rules, and one draw needn't show every extreme that they name: `routes`: each row names 8 different experts; in the tokens of one device no expert is named by more than 3 tokens, a bound that some block reaches.
All inputs are finite; a program needn't handle non-finite values. No bound on the sum of `lengths` on one device may be relied on, other than what follows from the above.
Results may differ from the reference program's by a relative error of at most 0.0057.
Values may be sent and summed in bfloat16 or wider, within the bound.
No kernel may reach another device: no remote copies, remote signals or barrier semaphores. Data moves between devices by JAX's collectives and lax.ppermute only.
A program may use at most 128 MiB of HBM per device.

```python
import math
import jax
import jax.numpy as jnp
import numpy as np
from jax import lax

D = 7168
FF = 2048
HEADS = 128
LATENT = 512
ROPE = 64
TOPK = 8
EXPERTS = 32
MOE_ROWS = 8
LMAX = 256
CAP = 3
TOKENS = 1024
ATT_TOTAL = 512
N_SEC = 2
N_DEV = 64


def cache_base(key):
    base = jax.random.uniform(key, (ATT_TOTAL, LMAX, LATENT + ROPE), jnp.float32, -1.7, 1.7)
    second = 0.99 * base[:, 0, :] + 0.3 * base[:, 1, :]
    return base.at[:, 1, :].set(second)


def draw_cache(key, part):
    base = cache_base(key)
    return base.astype(jnp.bfloat16)


def draw_queries(key, part):
    key = jax.random.fold_in(key, 7)
    shape = (ATT_TOTAL, HEADS, LATENT + ROPE)
    values = jnp.clip(jax.random.normal(key, shape, jnp.float32), -4.0, 4.0)
    return values.astype(jnp.bfloat16)


def with_ends(entries, own_key, low, largest):
    place = [jax.random.randint(jax.random.fold_in(own_key, axis), (), 0, length) for axis, length in enumerate(entries.shape)]
    widest = entries.shape.index(max(entries.shape))
    beside = place[:widest] + [(place[widest] + 1) % entries.shape[widest]] + place[widest + 1:]
    return entries.at[tuple(place)].set(low).at[tuple(beside)].set(largest)


def shard_levels(rng, dims, shards, low, high):
    def one(dim, parts):
        heights = jax.random.uniform(jax.random.fold_in(jax.random.fold_in(rng, 6), dim), (parts,), jnp.float32, low / len(shards), high / len(shards))
        return jnp.repeat(jnp.exp(heights), dims[dim] // parts).reshape((-1,) + (1,) * (len(dims) - dim - 1))

    factor_of = one(*shards[0])
    for cut in shards[1:]:
        factor_of = factor_of * one(*cut)
    return factor_of


def length_profile(amount, total, limit, skew):
    weights = [(1 << 20) // math.isqrt(grade ** skew) + 1 for grade in range(2, amount + 1)]
    rest, given = total - limit - (amount - 1), [1] * (amount - 1)
    while rest > 0:
        candidates = [i for i in range(amount - 1) if given[i] < limit]
        pool, remaining = sum([weights[i] for i in candidates]), rest
        for i in candidates:
            addition = min(limit - given[i], max(1, remaining * weights[i] // pool), rest)
            given[i] = given[i] + addition
            rest = rest - addition
    return np.array([limit] + given)


def ragged(rng, number_of, total, reach, lean):
    if number_of == 2:
        one = jax.random.randint(rng, (), max(1, total - reach), min(reach, total - 1) + 1)
        return jnp.stack([one, total - one])
    tallies = jnp.asarray(length_profile(number_of, total, reach, lean), jnp.int32)
    pairs = (number_of - 1) // 2
    source_of, receiver = tallies[1:1 + 2 * pairs:2], tallies[2:2 + 2 * pairs:2]
    slack = jnp.minimum(source_of - 1, reach - receiver)
    passed = jax.random.randint(jax.random.fold_in(rng, 1), (pairs,), 0, 1 << 20) % (slack + 1)
    tallies = tallies.at[1:1 + 2 * pairs:2].set(source_of - passed).at[2:2 + 2 * pairs:2].set(receiver + passed)
    return tallies[jax.random.permutation(jax.random.fold_in(rng, 2), number_of)]


def deal_out(key, own, number, rows, amount, top, limit, skew):
    sequence = jax.random.permutation(key, amount)
    heavy_load, common = portions_of(amount, rows * top, limit, skew, True), portions_of(amount, rows * top, limit, skew, False)
    places = jnp.arange(amount)

    def named(sizes, offset_by):
        used = int((sizes > 0).sum())
        fixed = max(1, used // 4)
        passed = fixed + (places - fixed + offset_by * (used - fixed)) % max(1, amount - fixed)
        return jnp.zeros((amount,), jnp.int32).at[sequence[jnp.where(places < fixed, places, passed)]].set(jnp.asarray(sizes, jnp.int32))

    sizes = jnp.where(number % 4 == 0, named(heavy_load, number // 4), named(common, number - number // 4 - 1))
    mixed = jax.random.permutation(jax.random.fold_in(own, 3), amount)
    giver, sink = mixed[0:amount // 2 * 2:2], mixed[1:amount // 2 * 2:2]
    slack = jnp.minimum(sizes[giver] - 1, limit - sizes[sink]) // 2
    slack = jnp.where((giver == sequence[0]) | (sink == sequence[0]) | (sizes[sink] == 0), 0, jnp.maximum(slack, 0))
    passed = jax.random.randint(jax.random.fold_in(own, 4), (amount // 2,), 0, 1 << 20) % (slack + 1)
    sizes = sizes.at[giver].add(-passed).at[sink].add(passed)
    members = jnp.searchsorted(jnp.cumsum(sizes), jnp.arange(rows * top), side="right").astype(jnp.int32)
    table = members.reshape(top, rows).T
    table = table[jax.random.permutation(jax.random.fold_in(own, 1), rows)]
    offset_by = jax.random.randint(jax.random.fold_in(own, 2), (rows, 1), 0, top)
    return jnp.take_along_axis(table, (jnp.arange(top)[None, :] + offset_by) % top, axis=1)


def portions_of(number_of, total, bound, lean, full):
    loads = [(1 << 20) // math.isqrt(grade ** lean) + 1 for grade in range(1, number_of + 1)]
    largest = bound if full else min(bound, max(-(-total // number_of), total * loads[0] // sum(loads)))
    least = 1 if total - largest >= number_of - 1 else 0
    counts, spare = [largest] + [least] * (number_of - 1), total - largest - least * (number_of - 1)
    while spare > 0:
        candidates = [i for i in range(1, number_of) if counts[i] < largest] or [i for i in range(1, number_of) if counts[i] < bound]
        whole, budget = sum([loads[i] for i in candidates]), spare
        for i in candidates:
            extra = min(bound - counts[i], max(1, budget * loads[i] // whole), spare)
            counts[i] = counts[i] + extra
            spare = spare - extra
    return np.array(counts)


def normal_values(key, shape, spread, reach, split=(), kind=jnp.bfloat16):
    entries = jax.random.normal(key, shape, jnp.float32) * spread
    if len(split) > 0:
        entries = shard_levels(key, shape, split, -0.22, 0.18) * entries
    return jnp.clip(entries, min=-reach, max=reach).astype(kind)


def setup_inputs(seed: int = 0) -> dict:
    streams_of = jax.random.split(jax.random.key(seed), 10)
    queries = draw_queries(jax.random.fold_in(streams_of[9], 71), 0)
    cache = draw_cache(jax.random.fold_in(streams_of[9], 71), 0)
    lengths = ragged(streams_of[2], ATT_TOTAL, ATT_TOTAL * LMAX // 2, LMAX, 1).astype(jnp.int32)
    hidden_rows = normal_values(streams_of[3], (TOKENS, D), 1.0, 6.0, ((0, 128),))
    routes_keys = jax.random.split(jax.random.fold_in(streams_of[4], 1), TOKENS // MOE_ROWS)
    routes_turns = jax.random.permutation(jax.random.fold_in(streams_of[4], 3), TOKENS // MOE_ROWS)
    routes = jax.vmap(lambda own, number: deal_out(jax.random.fold_in(streams_of[4], 2), own, number, MOE_ROWS, EXPERTS, TOPK, CAP, 2))(routes_keys, routes_turns).reshape((TOKENS, TOPK))
    gate_codes = with_ends(jax.random.randint(streams_of[5], (TOKENS, TOPK), 1, 65536), jax.random.fold_in(streams_of[5], 1), 1, 65535).astype(jnp.int32)
    placement = jax.random.permutation(streams_of[6], EXPERTS).astype(jnp.int32)
    w_gate_up = normal_values(streams_of[7], (2, D, EXPERTS * FF), D ** -0.5, 0.0625, ((2, 128),))
    w_down = normal_values(streams_of[8], (EXPERTS * FF, D), FF ** -0.5, 0.125, ((0, 128),))
    return dict(queries=queries, cache=cache, lengths=lengths, hidden_rows=hidden_rows, routes=routes, gate_codes=gate_codes, placement=placement, w_gate_up=w_gate_up, w_down=w_down)


SCORE_SCALE = 192.0 ** -0.5


def attend_row(items):
    query_row, key_rows, length = items
    scores = jnp.dot(query_row, key_rows.T, preferred_element_type=jnp.float32) * SCORE_SCALE
    places = jnp.arange(key_rows.shape[0], dtype=jnp.int32)
    scores = jnp.where(places[None, :] < length, scores, -1e30)
    peak_score = jnp.max(scores, axis=1, keepdims=True)
    raised = jnp.exp(scores - peak_score)
    weights = (raised / jnp.sum(raised, axis=1, keepdims=True)).astype(jnp.bfloat16)
    return jnp.dot(weights, key_rows[:, :LATENT], preferred_element_type=jnp.float32).astype(jnp.bfloat16)


def reference(queries, cache, lengths, hidden_rows, routes, gate_codes, placement, w_gate_up, w_down):
    context = lax.map(attend_row, (queries, cache, lengths))
    devices = N_SEC * N_DEV
    group = devices // EXPERTS
    slice_width = FF // group
    codes = gate_codes.astype(jnp.float32)
    gate_share = 2.5 * codes / jnp.sum(codes, axis=1, keepdims=True)
    expert_ids = jnp.arange(EXPERTS, dtype=jnp.int32)
    matched = (routes[:, :, None] == expert_ids[None, None, :]).astype(jnp.int32)
    owner_slot = jnp.sum(matched * placement[None, None, :], axis=2)
    on_slot = owner_slot[:, :, None] == expert_ids[None, None, :]
    weight = jnp.sum(jnp.where(on_slot, gate_share[:, :, None], 0.0), axis=1)
    member = jnp.sum(on_slot.astype(jnp.int32), axis=1)
    block_member = member.reshape(devices, MOE_ROWS, EXPERTS)
    position = jnp.cumsum(block_member, axis=1) - block_member
    capacity_ids = jnp.arange(CAP, dtype=jnp.int32)
    chosen = jnp.where((block_member[..., None] == 1) & (position[..., None] == capacity_ids), 1.0, 0.0).astype(jnp.float32)
    block_weight = weight.reshape(devices, MOE_ROWS, EXPERTS)
    row_blocks = hidden_rows.reshape(devices, MOE_ROWS, D).astype(jnp.float32)

    def per_slot(running, slot_id):
        picked = lax.dynamic_index_in_dim(chosen, slot_id, 2, keepdims=False)
        buffer = jnp.einsum("brc,brd->bcd", picked, row_blocks).astype(jnp.bfloat16).reshape(devices * CAP, D)
        start = (slot_id * FF).astype(jnp.int32)
        gate_cols = lax.dynamic_slice_in_dim(w_gate_up[0], start, FF, 1)
        up_cols = lax.dynamic_slice_in_dim(w_gate_up[1], start, FF, 1)
        down_rows = lax.dynamic_slice_in_dim(w_down, start, FF, 0)
        gate_act = jnp.dot(buffer, gate_cols, preferred_element_type=jnp.float32)
        up_act = jnp.dot(buffer, up_cols, preferred_element_type=jnp.float32)
        inner_act = (jax.nn.silu(gate_act) * up_act).astype(jnp.bfloat16)
        part_rows = jnp.einsum("pgs,gsd->pgd", inner_act.reshape(devices * CAP, group, slice_width).astype(jnp.float32), down_rows.reshape(group, slice_width, D).astype(jnp.float32))
        part_rows = lax.optimization_barrier(part_rows.astype(jnp.bfloat16)).astype(jnp.float32)
        summed = jnp.sum(part_rows, axis=1).reshape(devices, CAP, D)
        slot_weight = lax.dynamic_index_in_dim(block_weight, slot_id, 2, keepdims=False)
        factors = picked * slot_weight[:, :, None]
        running = running + jnp.einsum("brc,bcd->brd", factors, summed, precision=lax.Precision.HIGHEST)
        return running, None

    start_sum = jnp.zeros((devices, MOE_ROWS, D), jnp.float32)
    running, _ = lax.scan(per_slot, start_sum, jnp.arange(EXPERTS, dtype=jnp.int32))
    mixed = running.reshape(devices * MOE_ROWS, D).astype(jnp.bfloat16)
    return context, mixed
```

```python
import jax
import jax.numpy as jnp
from jax import lax
from jax.sharding import PartitionSpec as P

D = 7168
LATENT = 512
EXPERTS = 32
CAP = 3
ROWS = 8
SCORE_SCALE = 192.0 ** (-0.5)

AXES = ("sec", "dev")
GRAY = (0, 1, 3, 2)
DIMS = ((1, 2, 32, 8, 16, 4), (4, 8, 16, 2, 32, 1))
EDGES = (0, 2304, 4736, 7168)
TABLE = 128
GROUPS = 4
GROUP_TOKENS = 128
GROUP_ROWS = 48


def code_of(dev):
    y, x, z = dev // 16, (dev // 4) % 4, dev % 4
    return GRAY[z] | GRAY[x] << 2 | GRAY[y] << 4


def dev_of(code):
    return GRAY[code & 3] | GRAY[(code >> 2) & 3] << 2 | GRAY[(code >> 4) & 3] << 4


def exchange(rows, *dims):
    pairs = []
    for sec in range(2):
        mask = 0
        for d in dims:
            mask |= DIMS[sec][d]
        for dev in range(64):
            pairs.append((sec * 64 + dev, sec * 64 + dev_of(code_of(dev) ^ mask)))
    return lax.ppermute(rows, AXES, pairs)


def swap_cores(rows):
    return lax.ppermute(rows, "sec", [(0, 1), (1, 0)])


def attend(queries, cache, lengths):
    scores = (
        jnp.einsum("rhc,rlc->rhl", queries, cache, preferred_element_type=jnp.float32) * SCORE_SCALE
    )
    places = lax.broadcasted_iota(jnp.int32, scores.shape, 2)
    scores = jnp.where(places < lengths[:, None, None], scores, -1e30)
    peak_score = jnp.max(scores, axis=2, keepdims=True)
    raised = jnp.exp(scores - peak_score)
    weights = (raised / jnp.sum(raised, axis=2, keepdims=True)).astype(jnp.bfloat16)
    return jnp.einsum(
        "rhl,rlc->rhc", weights, cache[:, :, :LATENT], preferred_element_type=jnp.float32
    ).astype(jnp.bfloat16)


def route_table(routes, gate_codes, placement):
    codes = gate_codes.astype(jnp.float32)
    gate_share = 2.5 * codes / jnp.sum(codes, axis=1, keepdims=True)
    expert_ids = lax.broadcasted_iota(jnp.int32, (1, 1, EXPERTS), 2)
    matched = (routes[:, :, None] == expert_ids).astype(jnp.int32)
    owner_slot = jnp.sum(matched * placement[None, None, :], axis=2)
    on_slot = owner_slot[:, :, None] == expert_ids
    weight = jnp.sum(jnp.where(on_slot, gate_share[:, :, None], 0.0), axis=1)
    member = jnp.sum(on_slot.astype(jnp.int32), axis=1)
    rank = jnp.cumsum(member, axis=0) * member
    high = lax.reduce_precision(weight, 8, 7)
    low = lax.reduce_precision(weight - high, 8, 7)
    return jnp.concatenate(
        [rank.astype(jnp.float32), high, low, jnp.zeros_like(high)], axis=1
    ).astype(jnp.bfloat16)


def superblocks(rows):
    return rows.reshape(2, 2, 2, 64, rows.shape[-1])


def gather(stream):
    stream = jnp.concatenate(
        [stream, exchange(stream, 0), exchange(stream, 1), exchange(stream, 0, 1)]
    )
    stream = jnp.concatenate([stream, exchange(stream, 2)])
    width = stream.shape[1] // 3
    parts = [stream[:, i * width : (i + 1) * width] for i in range(3)]
    for step in range(3):
        parts = [
            jnp.concatenate([part, exchange(part, 3 + (i + step) % 3)])
            for i, part in enumerate(parts)
        ]
    out = []
    for i, part in enumerate(parts):
        names = [3 + (i + 2) % 3, 3 + (i + 1) % 3, 3 + i % 3]
        order = [names.index(5), names.index(4), names.index(3), 3, 4]
        out.append(superblocks(part).transpose(order).reshape(512, width))
    return out


def scatter(parts):
    for step in (2, 1, 0):
        new = []
        for i, part in enumerate(parts):
            left = part if step < 2 else superblocks(part)
            if step == 2:
                names = [5, 4, 3]
            else:
                names = [d for d in (5, 4, 3) if d in [3 + (i + s) % 3 for s in range(step + 1)]]
            axis = names.index(3 + (i + step) % 3)
            keep = lax.index_in_dim(left, 0, axis, keepdims=False)
            give = lax.index_in_dim(left, 1, axis, keepdims=False)
            shape = give.shape
            got = exchange(give.reshape(-1, shape[-1]), 3 + (i + step) % 3).reshape(shape)
            new.append((keep.astype(jnp.float32) + got.astype(jnp.float32)).astype(jnp.bfloat16))
        parts = new
    rows = jnp.concatenate(parts, axis=1)
    got = exchange(rows[32:], 2)
    rows = (rows[:32].astype(jnp.float32) + got.astype(jnp.float32)).astype(jnp.bfloat16)
    total = rows[:8].astype(jnp.float32)
    for block, dims in ((1, (0,)), (2, (1,)), (3, (0, 1))):
        total = total + exchange(rows[8 * block : 8 * block + 8], *dims).astype(jnp.float32)
    return total


def local(queries, cache, lengths, hidden_rows, routes, gate_codes, placement, w_gate_up, w_down):
    sec = lax.axis_index("sec")
    column = lax.axis_index("dev") // 4
    table = route_table(routes, gate_codes, placement)
    stream = jnp.concatenate(
        [hidden_rows[:, : EDGES[1]], table, hidden_rows[:, EDGES[1] :]], axis=1
    )
    context = attend(queries, cache, lengths)
    parts = gather(stream)
    tables = parts[0][:, EDGES[1] :]
    parts[0] = parts[0][:, : EDGES[1]]

    own_slot = sec * 16 + column
    sibling_slot = (1 - sec) * 16 + column
    slots = jnp.stack([own_slot, sibling_slot])
    picks = slots[None, :] + 32 * jnp.arange(3)[:, None]
    onehot = (lax.broadcasted_iota(jnp.int32, (3, 2, TABLE), 2) == picks[:, :, None]).astype(
        jnp.bfloat16
    )
    fields = jnp.einsum("fsc,tc->fst", onehot, tables, preferred_element_type=jnp.float32)
    fields = fields.reshape(3, 2, GROUPS, 1, GROUP_TOKENS)
    row_ids = lax.broadcasted_iota(jnp.int32, (1, 1, GROUP_ROWS, GROUP_TOKENS), 2)
    token_ids = lax.broadcasted_iota(jnp.int32, (1, 1, GROUP_ROWS, GROUP_TOKENS), 3)
    chosen = (row_ids // CAP == token_ids // ROWS) & (
        fields[0] == (row_ids % CAP + 1).astype(jnp.float32)
    )
    pick = chosen.astype(jnp.bfloat16)
    weigh = [
        jnp.where(chosen, fields[f], 0.0).astype(jnp.bfloat16) for f in (1, 2)
    ]

    rows = GROUPS * GROUP_ROWS
    gate_act = up_act = None
    for i, part in enumerate(parts):
        tokens = part.reshape(GROUPS, GROUP_TOKENS, -1)
        width = part.shape[1]
        send = jnp.einsum(
            "grt,gtd->grd", pick[1], tokens, preferred_element_type=jnp.float32
        ).astype(jnp.bfloat16)
        keep = jnp.einsum(
            "grt,gtd->grd", pick[0], tokens, preferred_element_type=jnp.float32
        ).astype(jnp.bfloat16)
        got = swap_cores(send.reshape(rows, width))
        work = jnp.concatenate([keep.reshape(rows, width), got])
        w_part = w_gate_up[:, EDGES[i] : EDGES[i + 1]]
        gate = jnp.dot(work, w_part[0], preferred_element_type=jnp.float32)
        up = jnp.dot(work, w_part[1], preferred_element_type=jnp.float32)
        gate_act = gate if gate_act is None else gate_act + gate
        up_act = up if up_act is None else up_act + up
    inner_act = (jax.nn.silu(gate_act) * up_act).astype(jnp.bfloat16)

    factors = jnp.concatenate([weigh[0][0], weigh[1][0], weigh[0][1], weigh[1][1]], axis=1)
    terms = []
    for i in range(3):
        partial = jnp.dot(
            inner_act, w_down[:, EDGES[i] : EDGES[i + 1]], preferred_element_type=jnp.float32
        ).astype(jnp.bfloat16)
        got = swap_cores(partial[rows:]).reshape(GROUPS, GROUP_ROWS, -1)
        mine = partial[:rows].reshape(GROUPS, GROUP_ROWS, -1)
        both = jnp.concatenate([mine, mine, got, got], axis=1)
        term = jnp.einsum("grt,grd->gtd", factors, both, preferred_element_type=jnp.float32)
        terms.append(term.astype(jnp.bfloat16).reshape(512, -1))
    mixed = scatter(terms).astype(jnp.bfloat16)
    return (context, mixed)


def solution(mesh):
    return jax.shard_map(
        local,
        mesh=mesh,
        in_specs=(
            P("dev", "sec", None),
            P("dev", None, None),
            P("dev"),
            P(("sec", "dev"), None),
            P(("sec", "dev"), None),
            P(("sec", "dev"), None),
            P(),
            P(None, None, ("sec", "dev")),
            P(("sec", "dev"), None),
        ),
        out_specs=(P("dev", "sec", None), P(("sec", "dev"), None)),
        check_vma=False,
    )
```

```python
import jax
import jax.numpy as jnp
from jax import lax
from jax.experimental import pallas as pl
from jax.sharding import PartitionSpec as P

D = 7168
LATENT = 512
EXPERTS = 32
CAP = 3
ROWS = 8
TOPK = 8
SCORE_SCALE = 192.0 ** (-0.5)

AXES = ("sec", "dev")
GRAY = (0, 1, 3, 2)
FIRST = ((1, 2, 32), (4, 8, 16))
SECOND = ((8, 16, 4), (2, 32, 1))
CUBE = 8
TABLE = 128
SLOT_ROWS = 24
EDGES = (0, 2304, 4736, 7168)


def code_of(dev):
    y, x, z = dev // 16, (dev // 4) % 4, dev % 4
    return GRAY[z] | GRAY[x] << 2 | GRAY[y] << 4


def dev_of(code):
    return GRAY[code & 3] | GRAY[(code >> 2) & 3] << 2 | GRAY[(code >> 4) & 3] << 4


def masks_of(bits):
    return [sum(bit for i, bit in enumerate(bits) if k >> i & 1) for k in range(CUBE)]


def cube_exchange(rows, cube):
    groups = []
    for sec in range(2):
        masks = masks_of(cube[sec])
        for base in range(64):
            if base & masks[-1] == 0:
                groups.append([sec * 64 + dev_of(base | mask) for mask in masks])
    return lax.all_to_all(rows, AXES, 0, 0, tiled=True, axis_index_groups=groups)


def swap_cores(rows):
    return lax.ppermute(rows, "sec", [(0, 1), (1, 0)])


def attend(queries, cache, lengths):
    scores = (
        jnp.einsum("rhc,rlc->rhl", queries, cache, preferred_element_type=jnp.float32) * SCORE_SCALE
    )
    places = lax.broadcasted_iota(jnp.int32, scores.shape, 2)
    scores = jnp.where(places < lengths[:, None, None], scores, -1e30)
    peak_score = jnp.max(scores, axis=2, keepdims=True)
    raised = jnp.exp(scores - peak_score)
    weights = (raised / jnp.sum(raised, axis=2, keepdims=True)).astype(jnp.bfloat16)
    return jnp.einsum(
        "rhl,rlc->rhc", weights, cache[:, :, :LATENT], preferred_element_type=jnp.float32
    ).astype(jnp.bfloat16)


def outgoing_kernel(hidden_ref, routes_ref, codes_ref, out_ref):
    codes = codes_ref[...].astype(jnp.float32)
    gates = 2.5 * codes / jnp.sum(codes, axis=1, keepdims=True)
    routes = routes_ref[...]
    lanes = lax.broadcasted_iota(jnp.int32, (ROWS, TABLE), 1)
    member = jnp.zeros((ROWS, TABLE), jnp.float32)
    table = jnp.zeros((ROWS, TABLE), jnp.float32)
    for k in range(TOPK):
        expert = routes[:, k : k + 1]
        member = jnp.where(lanes == expert, 1.0, member)
        table = jnp.where(lanes == expert + EXPERTS, gates[:, k : k + 1], table)
    rank = member
    for back in range(1, ROWS):
        rank = rank + jnp.concatenate(
            [jnp.zeros((back, TABLE), jnp.float32), member[: ROWS - back]], axis=0
        )
    table = (table + rank * member).astype(jnp.bfloat16)
    row = jnp.concatenate([hidden_ref[...], table], axis=1)
    out_ref[...] = jnp.concatenate([row] * CUBE, axis=0)


def outgoing_rows(hidden_rows, routes, gate_codes):
    return pl.pallas_call(
        outgoing_kernel,
        out_shape=jax.ShapeDtypeStruct((CUBE * ROWS, D + TABLE), jnp.bfloat16),
    )(hidden_rows, routes, gate_codes)


def columns_of_cube():
    sec, dev = lax.axis_index("sec"), lax.axis_index("dev")

    def gray(place):
        return place ^ (place >> 1)

    code = gray(dev % 4) | gray(dev // 4 % 4) << 2 | gray(dev // 16) << 4
    masks = jnp.where(
        sec == 0, jnp.asarray(masks_of(SECOND[0])), jnp.asarray(masks_of(SECOND[1]))
    ).astype(jnp.int32)
    codes = (code & ~masks[-1]) | masks
    return gray(codes >> 4) * 4 + gray((codes >> 2) & 3)


def picks_of(tables, experts):
    count, tokens = experts.shape[0], tables.shape[0]
    picks = experts[None, :] + EXPERTS * jnp.arange(2)[:, None]
    onehot = (lax.broadcasted_iota(jnp.int32, (2, count, TABLE), 2) == picks[:, :, None]).astype(
        jnp.bfloat16
    )
    fields = jnp.einsum("fsc,tc->fst", onehot, tables, preferred_element_type=jnp.float32)
    shape = (count, SLOT_ROWS, tokens)
    row_ids = lax.broadcasted_iota(jnp.int32, shape, 1)
    token_ids = lax.broadcasted_iota(jnp.int32, shape, 2)
    chosen = (row_ids // CAP == token_ids // ROWS) & (
        fields[0][:, None, :] == (row_ids % CAP + 1).astype(jnp.float32)
    )
    weighted = jnp.where(chosen, fields[1][:, None, :], 0.0)
    return tuple(
        a.astype(jnp.bfloat16).reshape(count * SLOT_ROWS, tokens) for a in (chosen, weighted)
    )


def local(queries, cache, lengths, hidden_rows, routes, gate_codes, placement, w_gate_up, w_down):
    sec = lax.axis_index("sec")
    x = cube_exchange(outgoing_rows(hidden_rows, routes, gate_codes), FIRST)

    columns = columns_of_cube()
    slots = jnp.stack([sec * 16 + columns, (1 - sec) * 16 + columns], axis=1).reshape(-1)
    expert_ids = lax.broadcasted_iota(jnp.int32, (2 * CUBE, EXPERTS), 1)
    experts = jnp.sum(jnp.where(placement[None, :] == slots[:, None], expert_ids, 0), axis=1)
    onehot, factors = picks_of(x[:, D:], experts)
    sent = jnp.dot(onehot, x[:, :D], preferred_element_type=jnp.float32).astype(jnp.bfloat16)
    arrived = cube_exchange(sent, SECOND).reshape(CUBE, 2, SLOT_ROWS, D)
    context = attend(queries, cache, lengths)

    count = CUBE * SLOT_ROWS
    gate_act = up_act = None
    for i in range(3):
        cols = slice(EDGES[i], EDGES[i + 1])
        mine, others = (arrived[:, k, :, cols].reshape(count, -1) for k in range(2))
        work = jnp.concatenate([mine, swap_cores(others)])
        gate = jnp.dot(work, w_gate_up[0, cols], preferred_element_type=jnp.float32)
        up = jnp.dot(work, w_gate_up[1, cols], preferred_element_type=jnp.float32)
        gate_act = gate if gate_act is None else gate_act + gate
        up_act = up if up_act is None else up_act + up
    inner_act = (jax.nn.silu(gate_act) * up_act).astype(jnp.bfloat16)

    back = jnp.zeros((CUBE, 2, SLOT_ROWS, D), jnp.bfloat16)
    for i in range(3):
        partial = jnp.dot(
            inner_act, w_down[:, EDGES[i] : EDGES[i + 1]], preferred_element_type=jnp.float32
        ).astype(jnp.bfloat16)
        partial, inner_act = lax.optimization_barrier((partial, inner_act))
        others, inner_act = lax.optimization_barrier((partial[count:], inner_act))
        for k, rows in enumerate((partial[:count], swap_cores(others))):
            back = lax.dynamic_update_slice(
                back, rows.reshape(CUBE, 1, SLOT_ROWS, -1), (0, k, 0, EDGES[i])
            )
    returned = cube_exchange(back.reshape(2 * count, D), SECOND)
    terms = jnp.einsum("rt,rd->td", factors, returned, preferred_element_type=jnp.float32)
    sums = cube_exchange(terms.astype(jnp.bfloat16), FIRST).reshape(CUBE, ROWS, D)
    mixed = jnp.sum(sums.astype(jnp.float32), axis=0).astype(jnp.bfloat16)
    return (context, mixed)


def solution(mesh):
    return jax.shard_map(
        local,
        mesh=mesh,
        in_specs=(
            P("dev", "sec", None),
            P("dev", None, None),
            P("dev"),
            P(("sec", "dev"), None),
            P(("sec", "dev"), None),
            P(("sec", "dev"), None),
            P(),
            P(None, None, ("sec", "dev")),
            P(("sec", "dev"), None),
        ),
        out_specs=(P("dev", "sec", None), P(("sec", "dev"), None)),
        check_vma=False,
    )
```

```python
import jax
import jax.numpy as jnp
from jax import lax
from jax.experimental import pallas as pl
from jax.sharding import PartitionSpec as P

D = 7168
LATENT = 512
EXPERTS = 32
CAP = 3
ROWS = 8
TOPK = 8
SCORE_SCALE = 192.0 ** (-0.5)

AXES = ("sec", "dev")
GRAY = (0, 1, 3, 2)
FIRST = ((1, 2, 32), (4, 8, 16))
SECOND = ((8, 16, 4), (2, 32, 1))
CUBE = 8
TABLE = 128
SLOT_ROWS = 24
EDGES = (0, 2560, 7168)
OUT_EDGES = (0, 2304, 4736, 7168)


def code_of(dev):
    y, x, z = dev // 16, (dev // 4) % 4, dev % 4
    return GRAY[z] | GRAY[x] << 2 | GRAY[y] << 4


def dev_of(code):
    return GRAY[code & 3] | GRAY[(code >> 2) & 3] << 2 | GRAY[(code >> 4) & 3] << 4


def masks_of(bits):
    return [sum(bit for i, bit in enumerate(bits) if k >> i & 1) for k in range(CUBE)]


def cube_exchange(rows, cube):
    groups = []
    for sec in range(2):
        masks = masks_of(cube[sec])
        for base in range(64):
            if base & masks[-1] == 0:
                groups.append([sec * 64 + dev_of(base | mask) for mask in masks])
    return lax.all_to_all(rows, AXES, 0, 0, tiled=True, axis_index_groups=groups)


def swap_cores(rows):
    return lax.ppermute(rows, "sec", [(0, 1), (1, 0)])


def attend(queries, cache, lengths):
    scores = (
        jnp.einsum("rhc,rlc->rhl", queries, cache, preferred_element_type=jnp.float32) * SCORE_SCALE
    )
    places = lax.broadcasted_iota(jnp.int32, scores.shape, 2)
    scores = jnp.where(places < lengths[:, None, None], scores, -1e30)
    peak_score = jnp.max(scores, axis=2, keepdims=True)
    raised = jnp.exp(scores - peak_score)
    weights = (raised / jnp.sum(raised, axis=2, keepdims=True)).astype(jnp.bfloat16)
    return jnp.einsum(
        "rhl,rlc->rhc", weights, cache[:, :, :LATENT], preferred_element_type=jnp.float32
    ).astype(jnp.bfloat16)


def outgoing_kernel(hidden_ref, routes_ref, codes_ref, out_ref):
    codes = codes_ref[...].astype(jnp.float32)
    gates = 2.5 * codes / jnp.sum(codes, axis=1, keepdims=True)
    routes = routes_ref[...]
    lanes = lax.broadcasted_iota(jnp.int32, (ROWS, TABLE), 1)
    member = jnp.zeros((ROWS, TABLE), jnp.float32)
    table = jnp.zeros((ROWS, TABLE), jnp.float32)
    for k in range(TOPK):
        expert = routes[:, k : k + 1]
        member = jnp.where(lanes == expert, 1.0, member)
        table = jnp.where(lanes == expert + EXPERTS, gates[:, k : k + 1], table)
    rank = member
    for back in range(1, ROWS):
        rank = rank + jnp.concatenate(
            [jnp.zeros((back, TABLE), jnp.float32), member[: ROWS - back]], axis=0
        )
    table = (table + rank * member).astype(jnp.bfloat16)
    row = jnp.concatenate([hidden_ref[...], table], axis=1)
    out_ref[...] = jnp.concatenate([row] * CUBE, axis=0)


def outgoing_rows(hidden_rows, routes, gate_codes):
    return pl.pallas_call(
        outgoing_kernel,
        out_shape=jax.ShapeDtypeStruct((CUBE * ROWS, D + TABLE), jnp.bfloat16),
    )(hidden_rows, routes, gate_codes)


def columns_of_cube():
    sec, dev = lax.axis_index("sec"), lax.axis_index("dev")

    def gray(place):
        return place ^ (place >> 1)

    code = gray(dev % 4) | gray(dev // 4 % 4) << 2 | gray(dev // 16) << 4
    masks = jnp.where(
        sec == 0, jnp.asarray(masks_of(SECOND[0])), jnp.asarray(masks_of(SECOND[1]))
    ).astype(jnp.int32)
    codes = (code & ~masks[-1]) | masks
    return gray(codes >> 4) * 4 + gray((codes >> 2) & 3)


def picks_of(tables, experts):
    count, tokens = experts.shape[0], tables.shape[0]
    picks = experts[None, :] + EXPERTS * jnp.arange(2)[:, None]
    onehot = (lax.broadcasted_iota(jnp.int32, (2, count, TABLE), 2) == picks[:, :, None]).astype(
        jnp.bfloat16
    )
    fields = jnp.einsum("fsc,tc->fst", onehot, tables, preferred_element_type=jnp.float32)
    shape = (count, SLOT_ROWS, tokens)
    row_ids = lax.broadcasted_iota(jnp.int32, shape, 1)
    token_ids = lax.broadcasted_iota(jnp.int32, shape, 2)
    chosen = (row_ids // CAP == token_ids // ROWS) & (
        fields[0][:, None, :] == (row_ids % CAP + 1).astype(jnp.float32)
    )
    weighted = jnp.where(chosen, fields[1][:, None, :], 0.0)
    return tuple(
        a.astype(jnp.bfloat16).reshape(count * SLOT_ROWS, tokens) for a in (chosen, weighted)
    )


def local(queries, cache, lengths, hidden_rows, routes, gate_codes, placement, w_gate_up, w_down):
    sec = lax.axis_index("sec")
    x = cube_exchange(outgoing_rows(hidden_rows, routes, gate_codes), FIRST)

    columns = columns_of_cube()
    slots = jnp.stack([sec * 16 + columns, (1 - sec) * 16 + columns], axis=1).reshape(-1)
    expert_ids = lax.broadcasted_iota(jnp.int32, (2 * CUBE, EXPERTS), 1)
    experts = jnp.sum(jnp.where(placement[None, :] == slots[:, None], expert_ids, 0), axis=1)
    onehot, factors = picks_of(x[:, D:], experts)
    sent = jnp.dot(onehot, x[:, :D], preferred_element_type=jnp.float32).astype(jnp.bfloat16)
    arrived = cube_exchange(sent, SECOND).reshape(CUBE, 2, SLOT_ROWS, D)
    context = attend(queries, cache, lengths)

    count = CUBE * SLOT_ROWS
    gate_act = up_act = None
    for i in range(2):
        cols = slice(EDGES[i], EDGES[i + 1])
        mine, others = (arrived[:, k, :, cols].reshape(count, -1) for k in range(2))
        work = jnp.concatenate([mine, swap_cores(others)])
        if i > 0:
            work, gate_act, up_act = lax.optimization_barrier((work, gate_act, up_act))
        gate = jnp.dot(work, w_gate_up[0, cols], preferred_element_type=jnp.float32)
        up = jnp.dot(work, w_gate_up[1, cols], preferred_element_type=jnp.float32)
        gate_act = gate if gate_act is None else gate_act + gate
        up_act = up if up_act is None else up_act + up
    inner_act = (jax.nn.silu(gate_act) * up_act).astype(jnp.bfloat16)

    back = jnp.zeros((CUBE, 2, SLOT_ROWS, D), jnp.bfloat16)
    for i in range(3):
        partial = jnp.dot(
            inner_act, w_down[:, OUT_EDGES[i] : OUT_EDGES[i + 1]], preferred_element_type=jnp.float32
        ).astype(jnp.bfloat16)
        partial, inner_act = lax.optimization_barrier((partial, inner_act))
        others, inner_act = lax.optimization_barrier((partial[count:], inner_act))
        for k, rows in enumerate((partial[:count], swap_cores(others))):
            back = lax.dynamic_update_slice(
                back, rows.reshape(CUBE, 1, SLOT_ROWS, -1), (0, k, 0, OUT_EDGES[i])
            )
    returned = cube_exchange(back.reshape(2 * count, D), SECOND)
    terms = jnp.einsum("rt,rd->td", factors, returned, preferred_element_type=jnp.float32)
    sums = cube_exchange(terms.astype(jnp.bfloat16), FIRST).reshape(CUBE, ROWS, D)
    mixed = jnp.sum(sums.astype(jnp.float32), axis=0).astype(jnp.bfloat16)
    return (context, mixed)


def solution(mesh):
    return jax.shard_map(
        local,
        mesh=mesh,
        in_specs=(
            P("dev", "sec", None),
            P("dev", None, None),
            P("dev"),
            P(("sec", "dev"), None),
            P(("sec", "dev"), None),
            P(("sec", "dev"), None),
            P(),
            P(None, None, ("sec", "dev")),
            P(("sec", "dev"), None),
        ),
        out_specs=(P("dev", "sec", None), P(("sec", "dev"), None)),
        check_vma=False,
    )
```

```python
import jax
import jax.numpy as jnp
from jax import lax
from jax.experimental import pallas as pl
from jax.experimental.pallas import tpu as pltpu
from jax.sharding import PartitionSpec as P

D = 7168
LATENT = 512
EXPERTS = 32
CAP = 3
ROWS = 8
TOPK = 8
SCORE_SCALE = 192.0 ** (-0.5)

AXES = ("sec", "dev")
GRAY = (0, 1, 3, 2)
FIRST = ((1, 2, 32), (4, 8, 16))
SECOND = ((8, 16, 4), (2, 32, 1))
CUBE = 8
TABLE = 128
SLOT_ROWS = 24
EDGES = (0, 2560, 7168)
OUT_EDGES = (0, 2816, 5632, 7168)


def code_of(dev):
    y, x, z = dev // 16, (dev // 4) % 4, dev % 4
    return GRAY[z] | GRAY[x] << 2 | GRAY[y] << 4


def dev_of(code):
    return GRAY[code & 3] | GRAY[(code >> 2) & 3] << 2 | GRAY[(code >> 4) & 3] << 4


def masks_of(bits):
    return [sum(bit for i, bit in enumerate(bits) if k >> i & 1) for k in range(CUBE)]


def cube_exchange(rows, cube):
    groups = []
    for sec in range(2):
        masks = masks_of(cube[sec])
        for base in range(64):
            if base & masks[-1] == 0:
                groups.append([sec * 64 + dev_of(base | mask) for mask in masks])
    return lax.all_to_all(rows, AXES, 0, 0, tiled=True, axis_index_groups=groups)


def swap_cores(rows):
    return lax.ppermute(rows, "sec", [(0, 1), (1, 0)])


def attend(queries, cache, lengths):
    scores = (
        jnp.einsum("rhc,rlc->rhl", queries, cache, preferred_element_type=jnp.float32) * SCORE_SCALE
    )
    places = lax.broadcasted_iota(jnp.int32, scores.shape, 2)
    scores = jnp.where(places < lengths[:, None, None], scores, -1e30)
    peak_score = jnp.max(scores, axis=2, keepdims=True)
    raised = jnp.exp(scores - peak_score)
    weights = (raised / jnp.sum(raised, axis=2, keepdims=True)).astype(jnp.bfloat16)
    return jnp.einsum(
        "rhl,rlc->rhc", weights, cache[:, :, :LATENT], preferred_element_type=jnp.float32
    ).astype(jnp.bfloat16)


def outgoing_kernel(hidden_ref, routes_ref, codes_ref, out_ref):
    codes = codes_ref[...].astype(jnp.float32)
    gates = 2.5 * codes / jnp.sum(codes, axis=1, keepdims=True)
    routes = routes_ref[...]
    lanes = lax.broadcasted_iota(jnp.int32, (ROWS, TABLE), 1)
    member = jnp.zeros((ROWS, TABLE), jnp.float32)
    table = jnp.zeros((ROWS, TABLE), jnp.float32)
    for k in range(TOPK):
        expert = routes[:, k : k + 1]
        member = jnp.where(lanes == expert, 1.0, member)
        table = jnp.where(lanes == expert + EXPERTS, gates[:, k : k + 1], table)
    rank = member
    for back in range(1, ROWS):
        rank = rank + jnp.concatenate(
            [jnp.zeros((back, TABLE), jnp.float32), member[: ROWS - back]], axis=0
        )
    table = (table + rank * member).astype(jnp.bfloat16)
    row = jnp.concatenate([hidden_ref[...], table], axis=1)
    out_ref[...] = jnp.concatenate([row] * CUBE, axis=0)


def outgoing_rows(hidden_rows, routes, gate_codes):
    return pl.pallas_call(
        outgoing_kernel,
        out_shape=jax.ShapeDtypeStruct((CUBE * ROWS, D + TABLE), jnp.bfloat16),
    )(hidden_rows, routes, gate_codes)


def columns_of_cube():
    sec, dev = lax.axis_index("sec"), lax.axis_index("dev")

    def gray(place):
        return place ^ (place >> 1)

    code = gray(dev % 4) | gray(dev // 4 % 4) << 2 | gray(dev // 16) << 4
    masks = jnp.where(
        sec == 0, jnp.asarray(masks_of(SECOND[0])), jnp.asarray(masks_of(SECOND[1]))
    ).astype(jnp.int32)
    codes = (code & ~masks[-1]) | masks
    return gray(codes >> 4) * 4 + gray((codes >> 2) & 3)


def picks_of(tables, experts):
    count, tokens = experts.shape[0], tables.shape[0]
    picks = experts[None, :] + EXPERTS * jnp.arange(2)[:, None]
    onehot = (lax.broadcasted_iota(jnp.int32, (2, count, TABLE), 2) == picks[:, :, None]).astype(
        jnp.bfloat16
    )
    fields = jnp.einsum("fsc,tc->fst", onehot, tables, preferred_element_type=jnp.float32)
    shape = (count, SLOT_ROWS, tokens)
    row_ids = lax.broadcasted_iota(jnp.int32, shape, 1)
    token_ids = lax.broadcasted_iota(jnp.int32, shape, 2)
    chosen = (row_ids // CAP == token_ids // ROWS) & (
        fields[0][:, None, :] == (row_ids % CAP + 1).astype(jnp.float32)
    )
    weighted = jnp.where(chosen, fields[1][:, None, :], 0.0)
    return tuple(
        a.astype(jnp.bfloat16).reshape(count * SLOT_ROWS, tokens) for a in (chosen, weighted)
    )


def spread_kernel(factors_ref, rows_ref, out_ref):
    out_ref[...] = jnp.dot(
        factors_ref[...], rows_ref[...], preferred_element_type=jnp.float32
    ).astype(out_ref.dtype)


def spread(factors, rows):
    tokens, count = factors.shape
    block = rows.shape[1] // 2
    return pl.pallas_call(
        spread_kernel,
        grid=(2,),
        in_specs=[
            pl.BlockSpec((tokens, count), lambda n: (0, 0)),
            pl.BlockSpec((count, block), lambda n: (0, n)),
        ],
        out_specs=pl.BlockSpec((tokens, block), lambda n: (0, n)),
        out_shape=jax.ShapeDtypeStruct((tokens, rows.shape[1]), jnp.bfloat16),
        compiler_params=pltpu.CompilerParams(vmem_limit_bytes=60 * 2**20),
    )(factors, rows)


def local(queries, cache, lengths, hidden_rows, routes, gate_codes, placement, w_gate_up, w_down):
    sec = lax.axis_index("sec")
    x = cube_exchange(outgoing_rows(hidden_rows, routes, gate_codes), FIRST)

    columns = columns_of_cube()
    slots = jnp.stack([sec * 16 + columns, (1 - sec) * 16 + columns], axis=1).reshape(-1)
    expert_ids = lax.broadcasted_iota(jnp.int32, (2 * CUBE, EXPERTS), 1)
    experts = jnp.sum(jnp.where(placement[None, :] == slots[:, None], expert_ids, 0), axis=1)
    onehot, factors = picks_of(x[:, D:], experts)
    sent = jnp.dot(onehot, x[:, :D], preferred_element_type=jnp.float32).astype(jnp.bfloat16)
    arrived = cube_exchange(sent, SECOND).reshape(CUBE, 2, SLOT_ROWS, D)
    context = attend(queries, cache, lengths)

    count = CUBE * SLOT_ROWS
    gate_act = up_act = None
    for i in range(2):
        cols = slice(EDGES[i], EDGES[i + 1])
        mine, others = (arrived[:, k, :, cols].reshape(count, -1) for k in range(2))
        work = jnp.concatenate([mine, swap_cores(others)])
        if i > 0:
            work, gate_act, up_act = lax.optimization_barrier((work, gate_act, up_act))
        gate = jnp.dot(work, w_gate_up[0, cols], preferred_element_type=jnp.float32)
        up = jnp.dot(work, w_gate_up[1, cols], preferred_element_type=jnp.float32)
        gate_act = gate if gate_act is None else gate_act + gate
        up_act = up if up_act is None else up_act + up
    inner_act = (jax.nn.silu(gate_act) * up_act).astype(jnp.bfloat16)

    back = jnp.zeros((CUBE, 2, SLOT_ROWS, D), jnp.bfloat16)
    for i in range(3):
        partial = jnp.dot(
            inner_act, w_down[:, OUT_EDGES[i] : OUT_EDGES[i + 1]], preferred_element_type=jnp.float32
        ).astype(jnp.bfloat16)
        partial, inner_act = lax.optimization_barrier((partial, inner_act))
        others, inner_act = lax.optimization_barrier((partial[count:], inner_act))
        for k, rows in enumerate((partial[:count], swap_cores(others))):
            back = lax.dynamic_update_slice(
                back, rows.reshape(CUBE, 1, SLOT_ROWS, -1), (0, k, 0, OUT_EDGES[i])
            )
    returned = cube_exchange(back.reshape(2 * count, D), SECOND)
    terms = spread(factors.T, returned)
    sums = cube_exchange(terms, FIRST).reshape(CUBE, ROWS, D)
    mixed = jnp.sum(sums.astype(jnp.float32), axis=0).astype(jnp.bfloat16)
    return (context, mixed)


def solution(mesh):
    return jax.shard_map(
        local,
        mesh=mesh,
        in_specs=(
            P("dev", "sec", None),
            P("dev", None, None),
            P("dev"),
            P(("sec", "dev"), None),
            P(("sec", "dev"), None),
            P(("sec", "dev"), None),
            P(),
            P(None, None, ("sec", "dev")),
            P(("sec", "dev"), None),
        ),
        out_specs=(P("dev", "sec", None), P(("sec", "dev"), None)),
        check_vma=False,
    )
```

```python
import jax
import jax.numpy as jnp
from jax import lax
from jax.experimental import pallas as pl
from jax.experimental.pallas import tpu as pltpu
from jax.sharding import PartitionSpec as P

D = 7168
LATENT = 512
EXPERTS = 32
CAP = 3
ROWS = 8
TOPK = 8
SCORE_SCALE = 192.0 ** (-0.5)

AXES = ("sec", "dev")
GRAY = (0, 1, 3, 2)
FIRST = ((1, 2, 32), (4, 8, 16))
SECOND = ((8, 16, 4), (2, 32, 1))
CUBE = 8
TABLE = 128
SLOT_ROWS = 24
EDGES = (0, 2560, 7168)
OUT_EDGES = (0, 2560, 5120, 7168)


def code_of(dev):
    y, x, z = dev // 16, (dev // 4) % 4, dev % 4
    return GRAY[z] | GRAY[x] << 2 | GRAY[y] << 4


def dev_of(code):
    return GRAY[code & 3] | GRAY[(code >> 2) & 3] << 2 | GRAY[(code >> 4) & 3] << 4


def masks_of(bits):
    return [sum(bit for i, bit in enumerate(bits) if k >> i & 1) for k in range(CUBE)]


def cube_exchange(rows, cube):
    groups = []
    for sec in range(2):
        masks = masks_of(cube[sec])
        for base in range(64):
            if base & masks[-1] == 0:
                groups.append([sec * 64 + dev_of(base | mask) for mask in masks])
    return lax.all_to_all(rows, AXES, 0, 0, tiled=True, axis_index_groups=groups)


def swap_cores(rows):
    return lax.ppermute(rows, "sec", [(0, 1), (1, 0)])


def attend(queries, cache, lengths):
    scores = (
        jnp.einsum("rhc,rlc->rhl", queries, cache, preferred_element_type=jnp.float32) * SCORE_SCALE
    )
    places = lax.broadcasted_iota(jnp.int32, scores.shape, 2)
    scores = jnp.where(places < lengths[:, None, None], scores, -1e30)
    peak_score = jnp.max(scores, axis=2, keepdims=True)
    raised = jnp.exp(scores - peak_score)
    weights = (raised / jnp.sum(raised, axis=2, keepdims=True)).astype(jnp.bfloat16)
    return jnp.einsum(
        "rhl,rlc->rhc", weights, cache[:, :, :LATENT], preferred_element_type=jnp.float32
    ).astype(jnp.bfloat16)


def outgoing_kernel(hidden_ref, routes_ref, codes_ref, out_ref):
    codes = codes_ref[...].astype(jnp.float32)
    gates = 2.5 * codes / jnp.sum(codes, axis=1, keepdims=True)
    routes = routes_ref[...]
    lanes = lax.broadcasted_iota(jnp.int32, (ROWS, TABLE), 1)
    member = jnp.zeros((ROWS, TABLE), jnp.float32)
    table = jnp.zeros((ROWS, TABLE), jnp.float32)
    for k in range(TOPK):
        expert = routes[:, k : k + 1]
        member = jnp.where(lanes == expert, 1.0, member)
        table = jnp.where(lanes == expert + EXPERTS, gates[:, k : k + 1], table)
    rank = member
    for back in range(1, ROWS):
        rank = rank + jnp.concatenate(
            [jnp.zeros((back, TABLE), jnp.float32), member[: ROWS - back]], axis=0
        )
    table = (table + rank * member).astype(jnp.bfloat16)
    row = jnp.concatenate([hidden_ref[...], table], axis=1)
    out_ref[...] = jnp.concatenate([row] * CUBE, axis=0)


def outgoing_rows(hidden_rows, routes, gate_codes):
    return pl.pallas_call(
        outgoing_kernel,
        out_shape=jax.ShapeDtypeStruct((CUBE * ROWS, D + TABLE), jnp.bfloat16),
    )(hidden_rows, routes, gate_codes)


def columns_of_cube():
    sec, dev = lax.axis_index("sec"), lax.axis_index("dev")

    def gray(place):
        return place ^ (place >> 1)

    code = gray(dev % 4) | gray(dev // 4 % 4) << 2 | gray(dev // 16) << 4
    masks = jnp.where(
        sec == 0, jnp.asarray(masks_of(SECOND[0])), jnp.asarray(masks_of(SECOND[1]))
    ).astype(jnp.int32)
    codes = (code & ~masks[-1]) | masks
    return gray(codes >> 4) * 4 + gray((codes >> 2) & 3)


def picks_of(tables, experts):
    count, tokens = experts.shape[0], tables.shape[0]
    picks = experts[None, :] + EXPERTS * jnp.arange(2)[:, None]
    onehot = (lax.broadcasted_iota(jnp.int32, (2, count, TABLE), 2) == picks[:, :, None]).astype(
        jnp.bfloat16
    )
    fields = jnp.einsum("fsc,tc->fst", onehot, tables, preferred_element_type=jnp.float32)
    shape = (count, SLOT_ROWS, tokens)
    row_ids = lax.broadcasted_iota(jnp.int32, shape, 1)
    token_ids = lax.broadcasted_iota(jnp.int32, shape, 2)
    chosen = (row_ids // CAP == token_ids // ROWS) & (
        fields[0][:, None, :] == (row_ids % CAP + 1).astype(jnp.float32)
    )
    weighted = jnp.where(chosen, fields[1][:, None, :], 0.0)
    return tuple(
        a.astype(jnp.bfloat16).reshape(count * SLOT_ROWS, tokens) for a in (chosen, weighted)
    )


def spread_kernel(factors_ref, rows_ref, out_ref):
    out_ref[...] = jnp.dot(
        factors_ref[...], rows_ref[...], preferred_element_type=jnp.float32
    ).astype(out_ref.dtype)


def spread(factors, rows):
    tokens, count = factors.shape
    block = rows.shape[1] // 2
    return pl.pallas_call(
        spread_kernel,
        grid=(2,),
        in_specs=[
            pl.BlockSpec((tokens, count), lambda n: (0, 0)),
            pl.BlockSpec((count, block), lambda n: (0, n)),
        ],
        out_specs=pl.BlockSpec((tokens, block), lambda n: (0, n)),
        out_shape=jax.ShapeDtypeStruct((tokens, rows.shape[1]), jnp.bfloat16),
        compiler_params=pltpu.CompilerParams(vmem_limit_bytes=60 * 2**20),
    )(factors, rows)


def local(queries, cache, lengths, hidden_rows, routes, gate_codes, placement, w_gate_up, w_down):
    sec = lax.axis_index("sec")
    x = cube_exchange(outgoing_rows(hidden_rows, routes, gate_codes), FIRST)

    columns = columns_of_cube()
    slots = jnp.stack([sec * 16 + columns, (1 - sec) * 16 + columns], axis=1).reshape(-1)
    expert_ids = lax.broadcasted_iota(jnp.int32, (2 * CUBE, EXPERTS), 1)
    experts = jnp.sum(jnp.where(placement[None, :] == slots[:, None], expert_ids, 0), axis=1)
    onehot, factors = picks_of(x[:, D:], experts)
    sent = jnp.dot(onehot, x[:, :D], preferred_element_type=jnp.float32).astype(jnp.bfloat16)
    arrived = cube_exchange(sent, SECOND).reshape(CUBE, 2, SLOT_ROWS, D)
    context = attend(queries, cache, lengths)

    count = CUBE * SLOT_ROWS
    gate_act = up_act = None
    for i in range(2):
        cols = slice(EDGES[i], EDGES[i + 1])
        mine, others = (arrived[:, k, :, cols].reshape(count, -1) for k in range(2))
        work = jnp.concatenate([mine, swap_cores(others)])
        if i > 0:
            work, gate_act, up_act = lax.optimization_barrier((work, gate_act, up_act))
        gate = jnp.dot(work, w_gate_up[0, cols], preferred_element_type=jnp.float32)
        up = jnp.dot(work, w_gate_up[1, cols], preferred_element_type=jnp.float32)
        gate_act = gate if gate_act is None else gate_act + gate
        up_act = up if up_act is None else up_act + up
    inner_act = (jax.nn.silu(gate_act) * up_act).astype(jnp.bfloat16)

    back = jnp.zeros((CUBE, 2, SLOT_ROWS, D), jnp.bfloat16)
    for i in range(3):
        partial = jnp.dot(
            inner_act, w_down[:, OUT_EDGES[i] : OUT_EDGES[i + 1]], preferred_element_type=jnp.float32
        ).astype(jnp.bfloat16)
        partial, inner_act = lax.optimization_barrier((partial, inner_act))
        others, inner_act = lax.optimization_barrier((partial[count:], inner_act))
        for k, rows in enumerate((partial[:count], swap_cores(others))):
            back = lax.dynamic_update_slice(
                back, rows.reshape(CUBE, 1, SLOT_ROWS, -1), (0, k, 0, OUT_EDGES[i])
            )
    returned = cube_exchange(back.reshape(2 * count, D), SECOND)
    terms = spread(factors.T, returned)
    sums = cube_exchange(terms, FIRST).reshape(CUBE, ROWS, D)
    mixed = jnp.sum(sums.astype(jnp.float32), axis=0).astype(jnp.bfloat16)
    return (context, mixed)


def solution(mesh):
    return jax.shard_map(
        local,
        mesh=mesh,
        in_specs=(
            P("dev", "sec", None),
            P("dev", None, None),
            P("dev"),
            P(("sec", "dev"), None),
            P(("sec", "dev"), None),
            P(("sec", "dev"), None),
            P(),
            P(None, None, ("sec", "dev")),
            P(("sec", "dev"), None),
        ),
        out_specs=(P("dev", "sec", None), P(("sec", "dev"), None)),
        check_vma=False,
    )
```
